512 devices in a mesh: tm: 16 (over z), space: 32 (over y, x, core).
Axes of the slice: x: 4, y: 4, z: 16, core: 2. Of those that a mesh axis runs over, the one named last changes fastest.
Arguments:
- displacements: bfloat16 [3, 16384, 16384], P(None, 'tm', 'space'), may hold values from -86.19596 to 86.19596
- block_place: int32 [128], replicated, may hold values from 0 to 127, as said below
- pair_list: int32 [384, 2], P('space'), may hold values from 0 to 127, as said below
- counts: int32 [32], P('space'), may hold values from 2 to 12, as said below
Outputs:
- covariance: float32 [384, 384, 384], P('tm', 'space')
The draws below stay inside these ranges and needn't reach their ends.
Inputs may be any that keep to these rules, and one draw needn't show every extreme that they name: Block k is stored at position block_place[k] with block_place[k] // 4 equal to k // 4; on each device's 4 positions it is a permutation. `pair_list`: row i belongs to spatial device i // 12; its owner block lies on that device; its partner differs from the owner and lies on the same device or on one of the two devices beside it along space, cyclically; among a device's rows in use, the partners on the device before it are one single block, named at least once, and likewise for the device after it. `counts`: rows at or beyond the count are ignored; some device uses all 12 rows.
All inputs are finite; a program needn't handle non-finite values.
Results may differ from the reference program's by a relative error of at most 0.0035.
Values may be sent and summed in bfloat16 or wider, within the bound.
A program may use at most 128 MiB of HBM per device.

```python
import jax
import jax.numpy as jnp
from jax import lax

FR_DEV = 1024
BLK_DEV = 4
P_CAP = 12
ATOMS_BLK = 128
WINDOW_FRAMES = 16384
ATOMS = 16384
N_TM = 16
N_SPACE = 32


def pair_counts(key):
    key_base = jax.random.fold_in(key, 11)
    spread = jax.random.randint(key_base, (N_SPACE,), 0, P_CAP)
    baseline_counts = 2 + spread * spread // P_CAP
    fullest = jax.random.randint(jax.random.fold_in(key, 12), (), 0, N_SPACE)
    return jnp.where(jnp.arange(N_SPACE) == fullest, P_CAP, baseline_counts).astype(jnp.int32)


def draw_counts(key, part):
    return pair_counts(key)


def draw_pair_list(key, part):
    used = pair_counts(key)
    key = jax.random.fold_in(key, 3)
    keys = jax.random.split(key, 7)
    device_ids = jnp.arange(N_SPACE, dtype=jnp.int32)[:, None]
    slot_index = jnp.arange(P_CAP, dtype=jnp.int32)[None, :]
    owner_local = jax.random.randint(keys[0], (N_SPACE, P_CAP), 0, BLK_DEV)
    owner_block = device_ids * BLK_DEV + owner_local
    left_block = (device_ids + N_SPACE - 1) % N_SPACE * BLK_DEV + jax.random.randint(keys[1], (N_SPACE, 1), 0, BLK_DEV)
    right_block = (device_ids + 1) % N_SPACE * BLK_DEV + jax.random.randint(keys[2], (N_SPACE, 1), 0, BLK_DEV)
    other_local = (owner_local + 1 + jax.random.randint(keys[3], (N_SPACE, P_CAP), 0, BLK_DEV - 1)) % BLK_DEV
    partner_kind = jax.random.randint(keys[4], (N_SPACE, P_CAP), 0, 3)
    limit = used[:, None]
    left_slot = jax.random.randint(keys[5], (N_SPACE, 1), 0, P_CAP) % limit
    right_slot = (left_slot + 1 + jax.random.randint(keys[6], (N_SPACE, 1), 0, P_CAP) % (limit - 1)) % limit
    partner_kind = jnp.where(slot_index == left_slot, 1, jnp.where(slot_index == right_slot, 2, partner_kind))
    partner_kind = jnp.where(slot_index < limit, partner_kind, 0)
    partner_block = jnp.where(partner_kind == 1, left_block, jnp.where(partner_kind == 2, right_block, device_ids * BLK_DEV + other_local))
    return jnp.stack([owner_block, partner_block], axis=-1).reshape(N_SPACE * P_CAP, 2).astype(jnp.int32)


def draw_block_place(key, part):
    key = jax.random.fold_in(key, 5)
    keys = jax.random.split(key, N_SPACE)
    orders = jax.vmap(lambda single: jax.random.permutation(single, BLK_DEV))(keys)
    device_ids = jnp.arange(N_SPACE, dtype=jnp.int32)[:, None]
    return (device_ids * BLK_DEV + orders).reshape(N_SPACE * BLK_DEV).astype(jnp.int32)


def draw_displacements(key, part):
    key = jax.random.fold_in(key, 7)
    key_speed, key_jitter, key_offset = jax.random.split(key, 3)
    shape = (3, WINDOW_FRAMES, ATOMS)
    time_ramp = (jnp.arange(WINDOW_FRAMES, dtype=jnp.float32) / WINDOW_FRAMES - 0.5)[None, :, None]
    velocity = jax.random.uniform(key_speed, (3, 1, ATOMS), jnp.float32, -6.0, 6.0)
    offsets = jax.random.uniform(key_offset, (3, 1, ATOMS), jnp.float32, -4.0, 4.0)
    noise_scale = WINDOW_FRAMES ** 0.25
    jitter = jnp.clip(jax.random.normal(key_jitter, shape, jnp.float32), -6.0, 6.0)
    return (offsets + velocity * time_ramp + noise_scale * jitter).astype(jnp.bfloat16)


def setup_inputs(seed: int = 0) -> dict:
    key_list = jax.random.split(jax.random.key(seed), 5)
    return {
        "displacements": draw_displacements(jax.random.fold_in(key_list[4], 71), 0),
        "block_place": draw_block_place(jax.random.fold_in(key_list[4], 71), 0),
        "pair_list": draw_pair_list(jax.random.fold_in(key_list[4], 71), 0),
        "counts": draw_counts(jax.random.fold_in(key_list[4], 71), 0),
    }


def reference(displacements, block_place, pair_list, counts):
    values = displacements.astype(jnp.float32)
    frame_mean = jnp.sum(values, axis=1, keepdims=True) / WINDOW_FRAMES
    centered = (values - frame_mean).astype(jnp.bfloat16)
    grouped = centered.reshape(3, N_TM, FR_DEV, centered.shape[2])
    span_width = 3 * ATOMS_BLK

    def block_matrix(block_id):
        begin = (block_place[block_id] * ATOMS_BLK).astype(jnp.int32)
        piece = lax.dynamic_slice_in_dim(grouped, begin, ATOMS_BLK, 3)
        return jnp.transpose(piece, (1, 2, 0, 3)).reshape(N_TM, FR_DEV, span_width).astype(jnp.float32)

    def single_pair(row_id):
        owner_displacement_matrix = block_matrix(pair_list[row_id, 0])
        partner_displacement_matrix = block_matrix(pair_list[row_id, 1])
        partial_covariance = jnp.einsum("iux,iub->ixb", owner_displacement_matrix, partner_displacement_matrix, precision=lax.Precision.HIGHEST) / WINDOW_FRAMES
        summed = jnp.sum(partial_covariance, axis=0)
        active = (row_id % P_CAP) < counts[row_id // P_CAP]
        return jnp.where(active, summed, jnp.zeros_like(summed))

    results = lax.map(single_pair, jnp.arange(N_SPACE * P_CAP, dtype=jnp.int32))
    return jnp.transpose(results, (1, 0, 2))
```

```python
import functools

import jax
import jax.numpy as jnp
from jax import lax
from jax.experimental import pallas as pl
from jax.experimental.pallas import tpu as pltpu
from jax.sharding import PartitionSpec as P

MESH = pl.DeviceIdType.MESH
BLK = 128
COMPS = 3
SPAN = COMPS * BLK
GROUP = 2
EARLY = 4


def plan(here, per_device, n_space, place_ref, rows_ref, counts_ref, slot_ref, owner_ref, partner_ref):
    slots = rows_ref.shape[0]
    before = lax.rem(here + n_space - 1, n_space)
    after = lax.rem(here + 1, n_space)
    count = counts_ref[0]
    base = here * per_device
    own_used = jnp.int32(0)
    far_used = jnp.int32(0)
    want_before = jnp.int32(0)
    want_after = jnp.int32(0)
    keys, places, firsts, owners, partners = [], [], [], [], []
    for i in range(slots):
        o, q = rows_ref[i, 0], rows_ref[i, 1]
        q_dev = q // per_device
        o_pos = jnp.clip(place_ref[o] - base, 0, per_device - 1)
        q_pos = jnp.clip(place_ref[q] - q_dev * per_device, 0, per_device - 1)
        is_own = q_dev == here
        is_before = q_dev == before
        active = i < count
        key = o * (n_space * per_device) + q
        place = jnp.where(is_own, own_used, slots - 1 - far_used)
        first = jnp.where(active, jnp.int32(1), jnp.int32(0))
        for j in range(i):
            same = key == keys[j]
            place = jnp.where(same, places[j], place)
            first = jnp.where(same, 0, first)
        own_used = own_used + jnp.where(is_own, first, 0)
        far_used = far_used + jnp.where(is_own, 0, first)
        want_before = jnp.where(active & is_before, q_pos, want_before)
        want_after = jnp.where(active & (q_dev == after), q_pos, want_after)
        keys.append(key)
        places.append(place)
        firsts.append(first)
        owners.append(o_pos)
        partners.append(jnp.where(is_own, q_pos, jnp.where(is_before, per_device, per_device + 1)))
        slot_ref[i] = jnp.clip(place, 0, slots - 1)
    for k in range(slots):
        owner_k, partner_k = jnp.int32(0), jnp.int32(0)
        for i in range(slots):
            mine = (firsts[i] == 1) & (places[i] == k)
            owner_k = jnp.where(mine, owners[i], owner_k)
            partner_k = jnp.where(mine, partners[i], partner_k)
        owner_ref[k] = owner_k
        partner_ref[k] = partner_k
    return want_before, want_after


def kernel(
    n_tm,
    n_space,
    x_hbm,
    place_ref,
    rows_ref,
    counts_ref,
    out_ref,
    x_ref,
    pool_ref,
    turned_ref,
    part_ref,
    done_ref,
    sums_ref,
    first_ref,
    half_ref,
    second_ref,
    mean_ref,
    near_mean_ref,
    ask_ref,
    asked_ref,
    halo_out_ref,
    halo_in_ref,
    send_ref,
    recv_ref,
    slot_ref,
    owner_ref,
    partner_ref,
    load_sems,
    mean_sems,
    near_sems,
    ask_sems,
    halo_sems,
    ring_sems,
):
    z = lax.axis_index("tm")
    s = lax.axis_index("space")
    frames = x_ref.shape[2]
    slots = part_ref.shape[0]
    per_device = turned_ref.shape[0]
    rows = SPAN // n_tm
    steps = n_tm // 2
    groups = slots // GROUP
    quads = n_tm // 4
    before = (lax.rem(s + n_space - 1, n_space))
    after = lax.rem(s + 1, n_space)
    up = lax.rem(z + 1, n_tm)
    down = lax.rem(z + n_tm - 1, n_tm)
    near_z = [(z // 4) * 4 + lax.rem(z + r, 4) for r in range(1, 4)]
    far_z = [lax.rem(z + 4 * r, n_tm) for r in range(1, quads)]
    partners = [(z, before), (z, after), (up, s), (down, s)]
    partners += [(other, s) for other in near_z + far_z]

    def load(p):
        return pltpu.make_async_copy(x_hbm.at[:, :, p * BLK : (p + 1) * BLK], x_ref.at[p], load_sems.at[p])

    for p in range(per_device):
        load(p).start()

    barrier = pltpu.get_barrier_semaphore()
    for who in partners:
        pl.semaphore_signal(barrier, inc=1, device_id=who, device_id_type=MESH)

    want_before, want_after = plan(
        s, per_device, n_space, place_ref, rows_ref, counts_ref, slot_ref, owner_ref, partner_ref
    )
    ask_ref[0] = jnp.full(ask_ref.shape[1:], want_before, jnp.int32)
    ask_ref[1] = jnp.full(ask_ref.shape[1:], want_after, jnp.int32)
    pl.semaphore_wait(barrier, len(partners))

    def ask(side):
        return pltpu.make_async_remote_copy(
            src_ref=ask_ref.at[side],
            dst_ref=asked_ref.at[1 - side],
            send_sem=ask_sems.at[0, side],
            recv_sem=ask_sems.at[1, 1 - side],
            device_id=(z, (before, after)[side]),
            device_id_type=MESH,
        )

    for side in range(2):
        ask(side).start()

    sums_ref[...] = jnp.zeros_like(sums_ref)
    for p in range(per_device):
        load(p).wait()
        for c in range(COMPS):
            total = jnp.sum(x_ref[p, c].astype(jnp.float32), axis=0, keepdims=True)
            sums_ref[c * per_device + p : c * per_device + p + 1, :] = total

    def exchange(level, src, dst, slot, who, r):
        return pltpu.make_async_remote_copy(
            src_ref=src,
            dst_ref=dst.at[slot],
            send_sem=mean_sems.at[level, 0, r],
            recv_sem=mean_sems.at[level, 1, r],
            device_id=(who, s),
            device_id_type=MESH,
        )

    z_low, z_high = lax.rem(z, 4), z // 4
    for r, who in enumerate(near_z):
        exchange(0, sums_ref, first_ref, z_low, who, r).start()

    def halo(side, c):
        return pltpu.make_async_remote_copy(
            src_ref=halo_out_ref.at[side, c],
            dst_ref=halo_in_ref.at[1 - side, c],
            send_sem=halo_sems.at[0, side, c],
            recv_sem=halo_sems.at[1, 1 - side, c],
            device_id=(z, (before, after)[side]),
            device_id_type=MESH,
        )

    for side in range(2):
        ask(1 - side).wait_recv()
        wanted = jnp.clip(jnp.max(asked_ref[side]), 0, per_device - 1)
        for c in range(COMPS):
            halo_out_ref[side, c] = x_ref[wanted, c]
            halo(side, c).start()

    for r, who in enumerate(near_z):
        exchange(0, sums_ref, first_ref, z_low, who, r).wait_recv()
    first_ref[z_low] = sums_ref[...]
    half_ref[...] = (first_ref[0] + first_ref[1]) + (first_ref[2] + first_ref[3])
    for r, who in enumerate(far_z):
        exchange(1, half_ref, second_ref, z_high, who, r).start()
    for r, who in enumerate(far_z):
        exchange(1, half_ref, second_ref, z_high, who, r).wait_recv()
    second_ref[z_high] = half_ref[...]
    mean_sum = second_ref[0]
    for g in range(1, quads):
        mean_sum = mean_sum + second_ref[g]
    mean_ref[...] = mean_sum * (1.0 / (frames * n_tm))

    def near(side):
        return pltpu.make_async_remote_copy(
            src_ref=mean_ref,
            dst_ref=near_mean_ref.at[1 - side],
            send_sem=near_sems.at[0, side],
            recv_sem=near_sems.at[1, 1 - side],
            device_id=(z, (before, after)[side]),
            device_id_type=MESH,
        )

    for side in range(2):
        near(side).start()

    def centre_own(p, _):
        for c in range(COMPS):
            mean = mean_ref[pl.ds(c * per_device + p, 1), :]
            centred = (x_ref[p, c].astype(jnp.float32) - mean).astype(jnp.bfloat16)
            pool_ref[p, :, c * BLK : (c + 1) * BLK] = centred
            turned_ref[p, c] = centred.T
        return 0

    lax.fori_loop(0, per_device, centre_own, 0)

    def product(k, _):
        owner, partner = owner_ref[k], partner_ref[k]
        for c in range(COMPS):
            part_ref[k, c * BLK : (c + 1) * BLK, :] = jnp.dot(
                turned_ref[owner, c], pool_ref[partner], preferred_element_type=jnp.float32
            )
        return 0

    def length(way, g):
        return steps - (g + way) % 2

    def hop(way, k, g):
        return pltpu.make_async_remote_copy(
            src_ref=send_ref.at[way, k, g],
            dst_ref=recv_ref.at[way, k, g],
            send_sem=ring_sems.at[0, way, k, g],
            recv_sem=ring_sems.at[1, way, k, g],
            device_id=((up, down)[way], s),
            device_id_type=MESH,
        )

    def local(d, g):
        block = part_ref[g * GROUP : (g + 1) * GROUP, pl.ds(pl.multiple_of(d * rows, rows), rows), :]
        return block.reshape(GROUP * rows, SPAN)

    def forward(k, g, fresh):
        for way in range(2):
            ahead = length(way, g) - k
            target = lax.rem(z + n_tm + (ahead if way == 0 else -ahead), n_tm)
            value = local(target, g)
            if not fresh:
                hop(way, k - 1, g).wait_recv()
                value = value + recv_ref[way, k - 1, g].astype(jnp.float32)
            send_ref[way, k, g] = value.astype(jnp.bfloat16)
            hop(way, k, g).start()

    early = EARLY // GROUP
    for g in range(early):
        lax.fori_loop(g * GROUP, (g + 1) * GROUP, product, 0)
        forward(0, g, True)
    for g in range(early):
        forward(1, g, False)

    for side in range(2):
        near(side).wait_recv()
    for side in range(2):
        wanted = (want_before, want_after)[side]
        for c in range(COMPS):
            halo(1 - side, c).wait_recv()
            mean = near_mean_ref[side, c * per_device + wanted][None, :]
            centred = (halo_in_ref[side, c].astype(jnp.float32) - mean).astype(jnp.bfloat16)
            pool_ref[per_device + side, :, c * BLK : (c + 1) * BLK] = centred

    for g in range(early, groups):
        lax.fori_loop(g * GROUP, (g + 1) * GROUP, product, 0)
        forward(0, g, True)
    for g in range(early, groups):
        forward(1, g, False)

    def middle(k, _):
        for g in range(groups):
            forward(k, g, False)
        return 0

    lax.fori_loop(2, steps - 1, middle, 0)

    for g in range(groups):
        way = g % 2
        last = steps - 1
        target = up if way == 0 else down
        hop(way, last - 1, g).wait_recv()
        value = local(target, g) + recv_ref[way, last - 1, g].astype(jnp.float32)
        send_ref[way, last, g] = value.astype(jnp.bfloat16)
        hop(way, last, g).start()
    for g in range(groups):
        value = local(z, g)
        for way in (1 - g % 2, g % 2):
            last = length(way, g) - 1
            hop(way, last, g).wait_recv()
            value = value + recv_ref[way, last, g].astype(jnp.float32)
        done_ref[g * GROUP : (g + 1) * GROUP] = value.reshape(GROUP, rows, SPAN)

    scale = 1.0 / (frames * n_tm)
    for i in range(slots):
        weight = jnp.where(i < counts_ref[0], jnp.float32(scale), jnp.float32(0.0))
        out_ref[i] = done_ref[slot_ref[i]] * weight

    for side in range(2):
        ask(side).wait_send()
        near(side).wait_send()
        for c in range(COMPS):
            halo(side, c).wait_send()
    for r, who in enumerate(near_z):
        exchange(0, sums_ref, first_ref, z_low, who, r).wait_send()
    for r, who in enumerate(far_z):
        exchange(1, half_ref, second_ref, z_high, who, r).wait_send()

    def drain(k, _):
        for g in range(groups):
            for way in range(2):
                hop(way, k, g).wait_send()
        return 0

    lax.fori_loop(0, steps - 1, drain, 0)
    for g in range(groups):
        hop(g % 2, steps - 1, g).wait_send()


def body(n_tm, n_space, displacements, block_place, pair_list, counts):
    frames, atoms = displacements.shape[1:]
    per_device = atoms // BLK
    slots = pair_list.shape[0]
    rows = SPAN // n_tm
    steps, groups = n_tm // 2, slots // GROUP
    bf16, f32, i32 = jnp.bfloat16, jnp.float32, jnp.int32
    smem = pl.BlockSpec(memory_space=pltpu.SMEM)
    result = pl.pallas_call(
        functools.partial(kernel, n_tm, n_space),
        out_shape=jax.ShapeDtypeStruct((slots, rows, SPAN), f32),
        in_specs=[pl.BlockSpec(memory_space=pl.ANY), smem, smem, smem],
        out_specs=pl.BlockSpec(memory_space=pltpu.VMEM),
        scratch_shapes=[
            pltpu.VMEM((per_device, COMPS, frames, BLK), bf16),
            pltpu.VMEM((per_device + 2, frames, SPAN), bf16),
            pltpu.VMEM((per_device, COMPS, BLK, frames), bf16),
            pltpu.VMEM((slots, SPAN, SPAN), f32),
            pltpu.VMEM((slots, rows, SPAN), f32),
            pltpu.VMEM((16, BLK), f32),
            pltpu.VMEM((4, 16, BLK), f32),
            pltpu.VMEM((16, BLK), f32),
            pltpu.VMEM((n_tm // 4, 16, BLK), f32),
            pltpu.VMEM((16, BLK), f32),
            pltpu.VMEM((2, 16, BLK), f32),
            pltpu.VMEM((2, 8, BLK), i32),
            pltpu.VMEM((2, 8, BLK), i32),
            pltpu.VMEM((2, COMPS, frames, BLK), bf16),
            pltpu.VMEM((2, COMPS, frames, BLK), bf16),
            pltpu.VMEM((2, steps, groups, GROUP * rows, SPAN), bf16),
            pltpu.VMEM((2, steps, groups, GROUP * rows, SPAN), bf16),
            pltpu.SMEM((slots,), i32),
            pltpu.SMEM((slots,), i32),
            pltpu.SMEM((slots,), i32),
            pltpu.SemaphoreType.DMA((per_device,)),
            pltpu.SemaphoreType.DMA((2, 2, 3)),
            pltpu.SemaphoreType.DMA((2, 2)),
            pltpu.SemaphoreType.DMA((2, 2)),
            pltpu.SemaphoreType.DMA((2, 2, COMPS)),
            pltpu.SemaphoreType.DMA((2, 2, steps, groups)),
        ],
        compiler_params=pltpu.CompilerParams(
            collective_id=0, has_side_effects=True, vmem_limit_bytes=56 * 1024 * 1024
        ),
    )(displacements, block_place, pair_list, counts)
    return jnp.transpose(result, (1, 0, 2))


def solution(mesh):
    in_specs = (P(None, "tm", "space"), P(), P("space", None), P("space"))
    return jax.shard_map(
        functools.partial(body, mesh.shape["tm"], mesh.shape["space"]),
        mesh=mesh,
        in_specs=in_specs,
        out_specs=P("tm", "space", None),
        check_vma=False,
    )
```
